512 devices in a mesh: row: 16 (over z), col: 32 (over y, x, core).
Axes of the slice: x: 4, y: 4, z: 16, core: 2. Of those that a mesh axis runs over, the one named last changes fastest.
Arguments:
- counts: int32 [16, 32], P('row', 'col'), may hold values from 1 to 16, as said below
- block_rows: int32 [16, 32, 16], P('row', 'col'), may hold values from 0 to 31, as said below
- block_cols: int32 [16, 32, 16], P('row', 'col'), may hold values from 0 to 15, as said below
- values: bfloat16 [16, 32, 16, 128, 128], P('row', 'col'), may hold values from -0.1875 to 0.1875
- start_block: float32 [64, 65536], P(None, ('row', 'col')), may hold values from -6 to 6
Outputs:
- diag_blocks: float32 [4, 64, 64], replicated
- off_blocks: float32 [4, 64, 64], replicated
- next_basis: float32 [64, 65536], P(None, ('row', 'col'))
The draws below stay inside these ranges and needn't reach their ends.
Inputs may be any that keep to these rules, and one draw needn't show every extreme that they name: Each tile has 16 slots; only the first counts[r, c] are live. In every draw some tile has all 16 live. `block_rows`: block row within the tile's row tile; the global block row of a stored block never exceeds its global block column. `block_cols`: index r2 of the block column r2 * 32 + c of tile (r, c); r2 >= r.
All inputs are finite; a program needn't handle non-finite values.
Results may differ from the reference program's by a relative error of at most 0.04.
Values may be sent and summed in bfloat16 or wider, within the bound.
A program may use at most 64 MiB of HBM per device.

```python
import jax
import jax.numpy as jnp
from jax import lax

BLOCK = 64
EDGE = 128
CAP = 16
STEPS = 4
NODES = 65536
N_ROW = 16
N_COL = 32


def tile_pattern(key):
    key = jax.random.fold_in(key, 23)
    key_far, key_near = jax.random.split(key)
    grid_shape = (N_ROW, N_COL, CAP)
    tile_row = lax.broadcasted_iota(jnp.int32, grid_shape, 0)
    tile_col = lax.broadcasted_iota(jnp.int32, grid_shape, 1)
    far_tile = tile_row + jax.random.randint(key_far, grid_shape, 0, N_ROW - tile_row)
    row_limit = jnp.where(far_tile > tile_row, N_COL, tile_col + 1)
    near_row = jax.random.randint(key_near, grid_shape, 0, row_limit)
    return (near_row.astype(jnp.int32), far_tile.astype(jnp.int32))


def draw_block_rows(key, part):
    near_row, far_tile = tile_pattern(key)
    return near_row


def draw_block_cols(key, part):
    near_row, far_tile = tile_pattern(key)
    return far_tile


def draw_counts(key, part):
    key = jax.random.fold_in(key, 3)
    key_one, key_two, key_pick = jax.random.split(key, 3)
    grid_shape = (N_ROW * N_COL,)
    factor_one = jax.random.randint(key_one, grid_shape, 0, CAP)
    factor_two = jax.random.randint(key_two, grid_shape, 0, CAP)
    loads = CAP // 3 + 2 * factor_one * factor_two // (3 * CAP)
    chosen = jax.random.randint(key_pick, (), 0, N_ROW * N_COL)
    position = jnp.arange(N_ROW * N_COL, dtype=jnp.int32)
    loads = jnp.where(position == chosen, CAP, loads)
    return loads.astype(jnp.int32).reshape(N_ROW, N_COL)


def steps_of(own_key, extent, shards, smallest, top_value):
    factor_of, own = 1.0, jax.random.fold_in(own_key, 6)
    for axis_at, blocks in shards:
        draws = jnp.exp(jax.random.uniform(jax.random.fold_in(own, axis_at), (blocks,), jnp.float32, smallest / len(shards), top_value / len(shards)))
        factor_of = factor_of * jnp.repeat(draws, extent[axis_at] // blocks).reshape([-1 if axis == axis_at else 1 for axis in range(len(extent))])
    return factor_of


def bell_draw(stream_key, shape, scale, reach, shards=(), kind=jnp.bfloat16):
    array = jax.random.normal(stream_key, shape, jnp.float32) * scale
    if len(shards) > 0:
        array = steps_of(stream_key, shape, shards, -0.22, 0.18) * array
    return jnp.clip(array, min=-reach, max=reach).astype(kind)


def setup_inputs(seed: int = 0) -> dict:
    arg_keys = jax.random.split(jax.random.key(seed), 6)
    counts = draw_counts(jax.random.fold_in(arg_keys[5], 71), 0)
    block_rows = draw_block_rows(jax.random.fold_in(arg_keys[5], 71), 0)
    block_cols = draw_block_cols(jax.random.fold_in(arg_keys[5], 71), 0)
    values = bell_draw(arg_keys[3], (N_ROW, N_COL, CAP, EDGE, EDGE), (CAP * EDGE // 2) ** -0.5, 0.1875, ((0, 16), (1, 32)))
    start_block = bell_draw(arg_keys[4], (BLOCK, NODES), 1.0, 6.0, ((1, 512),), jnp.float32)
    return {"counts": counts, "block_rows": block_rows, "block_cols": block_cols, "values": values, "start_block": start_block}


exact_mode = lax.Precision.HIGHEST

def full_dot(left, right):
    return jnp.dot(left.astype(jnp.float32), right.astype(jnp.float32), precision=exact_mode, preferred_element_type=jnp.float32)

def outer_gram(left, right):
    return lax.dot_general(left.astype(jnp.float32), right.astype(jnp.float32), (((1,), (1,)), ((), ())), precision=exact_mode, preferred_element_type=jnp.float32)

def tile_terms(vectors, tile_index, live_count, row_slots, col_slots, tile_blocks):
    tile_row = tile_index // N_COL
    tile_col = tile_index % N_COL
    row_inputs = lax.dynamic_index_in_dim(vectors, tile_row, 1, keepdims=False)
    col_inputs = lax.dynamic_index_in_dim(vectors, tile_col, 2, keepdims=False)
    live_mask = (jnp.arange(CAP, dtype=jnp.int32) < live_count).astype(jnp.float32)
    row_onehot = (row_slots[:, None] == jnp.arange(N_COL, dtype=jnp.int32)[None, :]).astype(jnp.float32) * live_mask[:, None]
    col_onehot = (col_slots[:, None] == jnp.arange(N_ROW, dtype=jnp.int32)[None, :]).astype(jnp.float32) * live_mask[:, None]
    picked_cols = jnp.take(col_inputs, col_slots, axis=1).astype(jnp.float32)
    picked_rows = jnp.take(row_inputs, row_slots, axis=1).astype(jnp.float32)
    block_wide = tile_blocks.astype(jnp.float32)
    upper_term = jnp.einsum('dkj,kij->dki', picked_cols, block_wide, precision=exact_mode)
    lower_term = jnp.einsum('dki,kij->dkj', picked_rows, block_wide, precision=exact_mode)
    row_part = jnp.einsum('dki,kr->dri', upper_term, row_onehot, precision=exact_mode)
    col_part = jnp.einsum('dkj,kc->dcj', lower_term, col_onehot, precision=exact_mode)
    return (row_part.astype(jnp.bfloat16), col_part.astype(jnp.bfloat16))

def apply_operator(current, counts, block_rows, block_cols, values):
    vectors = current.astype(jnp.bfloat16).reshape(BLOCK, N_ROW, N_COL, EDGE)
    tile_total = N_ROW * N_COL

    def one_tile(inputs):
        tile_index, live_count, row_slots, col_slots, tile_blocks = inputs
        return tile_terms(vectors, tile_index, live_count, row_slots, col_slots, tile_blocks)
    row_parts, col_parts = lax.map(one_tile, (jnp.arange(tile_total, dtype=jnp.int32), counts.reshape(tile_total), block_rows.reshape(tile_total, CAP), block_cols.reshape(tile_total, CAP), values.reshape(tile_total, CAP, EDGE, EDGE)))
    row_sum = jnp.sum(row_parts.astype(jnp.float32).reshape(N_ROW, N_COL, BLOCK, N_COL, EDGE), axis=1)
    row_sum = jnp.transpose(row_sum, (1, 0, 2, 3))
    col_sum = jnp.sum(col_parts.astype(jnp.float32).reshape(N_ROW, N_COL, BLOCK, N_ROW, EDGE), axis=0)
    col_sum = jnp.transpose(col_sum, (1, 2, 0, 3))
    return current - (row_sum + col_sum).reshape(BLOCK, NODES)

def reference(counts, block_rows, block_cols, values, start_block):
    factor = jnp.linalg.cholesky(outer_gram(start_block, start_block))
    current = lax.linalg.triangular_solve(factor, start_block, left_side=True, lower=True)
    previous = None
    link_factor = factor
    diag_list = []
    link_list = []
    for turn_index in range(STEPS):
        image = apply_operator(current, counts, block_rows, block_cols, values)
        if previous is not None:
            image = image - full_dot(link_factor.T, previous)
        diag_block = outer_gram(image, current)
        image = image - full_dot(diag_block, current)
        link_factor = jnp.linalg.cholesky(outer_gram(image, image))
        next_rows = lax.linalg.triangular_solve(link_factor, image, left_side=True, lower=True)
        diag_list.append(diag_block)
        link_list.append(link_factor)
        previous = current
        current = next_rows
    return (jnp.stack(diag_list), jnp.stack(link_list), current)
```

```python
import functools

import jax
import jax.numpy as jnp
from jax import lax
from jax.experimental import pallas as pl
from jax.experimental.pallas import tpu as pltpu
from jax.sharding import PartitionSpec as P

STEPS = 4
HI = lax.Precision.HIGHEST
F32 = jnp.float32
BF = jnp.bfloat16
MESH = pl.DeviceIdType.MESH


def mm(a, b):
    return lax.dot_general(
        a, b, (((1,), (0,)), ((), ())), precision=HI, preferred_element_type=F32
    )


def mm_nt(a, b):
    return lax.dot_general(
        a, b, (((1,), (1,)), ((), ())), precision=HI, preferred_element_type=F32
    )


def factor(gram):
    n = gram.shape[0]
    row = lax.broadcasted_iota(jnp.int32, (n, 2 * n), 0)
    lane = lax.broadcasted_iota(jnp.int32, (n, 2 * n), 1)
    eye = (row[:, :n] == lane[:, :n]).astype(F32)
    m = jnp.concatenate([gram, eye], axis=1)

    def body(k, m):
        pivot_row = jnp.sum(jnp.where(row == k, m, 0.0), axis=0, keepdims=True)
        at_k = lane == k
        col = jnp.sum(jnp.where(at_k, m, 0.0), axis=1, keepdims=True)
        pivot = jnp.sum(
            jnp.where(at_k[:1], pivot_row, 0.0), axis=1, keepdims=True
        )
        mult = jnp.where(row[:, :1] > k, col / pivot, 0.0)
        return m - mult * pivot_row

    m = lax.fori_loop(0, n, body, m)
    diag = jnp.sum(jnp.where(row == lane, m, 0.0), axis=1, keepdims=True)
    m = m / jnp.sqrt(diag)
    upper = jnp.where(lane[:, :n] >= row[:, :n], m[:, :n], 0.0)
    return upper, m[:, n:]


def kernel(
    nr,
    nc,
    tab,
    vals,
    start,
    diag_o,
    off_o,
    basis_o,
    vals_t,
    xcol,
    xrow,
    wcol,
    wrow,
    scol,
    srow,
    pcol,
    prow,
    rcol,
    rrow,
    ga,
    g1,
    g2,
    g3,
    q_s,
    qs_s,
    qp_s,
    v_s,
    e_s,
    ax_send,
    ax_recv,
    ay_send,
    ay_recv,
    bx_send,
    bx_recv,
    by_send,
    by_recv,
    g1_send,
    g1_recv,
    g2_send,
    g2_recv,
    g3_send,
    g3_recv,
):
    cap = vals.shape[0]
    width = start.shape[0]
    part = width // nc
    r = lax.axis_index("row")
    c = lax.axis_index("col")

    def on_col(i):
        return lax.rem(r + i, nr)

    def on_row(i):
        return lax.rem(c + i, nc)

    barrier = pltpu.get_barrier_semaphore()

    @pl.loop(1, nr)
    def _(i):
        pl.semaphore_signal(
            barrier, inc=1, device_id=(on_col(i), c), device_id_type=MESH
        )

    @pl.loop(1, nc)
    def _(i):
        pl.semaphore_signal(
            barrier, inc=1, device_id=(r, on_row(i)), device_id_type=MESH
        )

    def ag_col(par, to, slot):
        return pltpu.make_async_remote_copy(
            src_ref=xcol.at[par, r],
            dst_ref=xcol.at[par, slot],
            send_sem=ax_send.at[to],
            recv_sem=ax_recv.at[par, slot],
            device_id=(to, c),
            device_id_type=MESH,
        )

    def ag_row(par, to, slot):
        return pltpu.make_async_remote_copy(
            src_ref=xrow.at[par, c],
            dst_ref=xrow.at[par, slot],
            send_sem=ay_send.at[to],
            recv_sem=ay_recv.at[par, slot],
            device_id=(r, to),
            device_id_type=MESH,
        )

    def rs_col(par, to, slot):
        return pltpu.make_async_remote_copy(
            src_ref=pcol.at[to],
            dst_ref=rcol.at[par, slot],
            send_sem=bx_send.at[to],
            recv_sem=bx_recv.at[par, slot],
            device_id=(to, c),
            device_id_type=MESH,
        )

    def rs_row(par, to, slot):
        return pltpu.make_async_remote_copy(
            src_ref=prow.at[to],
            dst_ref=rrow.at[par, slot],
            send_sem=by_send.at[to],
            recv_sem=by_recv.at[par, slot],
            device_id=(r, to),
            device_id_type=MESH,
        )

    def gram_1(par, to, slot):
        return pltpu.make_async_remote_copy(
            src_ref=ga.at[to],
            dst_ref=g1.at[par, slot],
            send_sem=g1_send.at[to],
            recv_sem=g1_recv.at[par, slot],
            device_id=(r, to),
            device_id_type=MESH,
        )

    def gram_2(par, to, slot):
        return pltpu.make_async_remote_copy(
            src_ref=g2.at[par, r],
            dst_ref=g2.at[par, slot],
            send_sem=g2_send.at[to],
            recv_sem=g2_recv.at[par, slot],
            device_id=(to, c),
            device_id_type=MESH,
        )

    def gram_3(par, to, slot):
        return pltpu.make_async_remote_copy(
            src_ref=g3.at[par, c],
            dst_ref=g3.at[par, slot],
            send_sem=g3_send.at[to],
            recv_sem=g3_recv.at[par, slot],
            device_id=(r, to),
            device_id_type=MESH,
        )

    def send_all(copy, par, count, at, me):
        @pl.loop(1, count)
        def _(i):
            copy(par, at(i), me).start()

    def recv_all(copy, par, count, at):
        @pl.loop(1, count)
        def _(i):
            copy(par, at(i), at(i)).wait_recv()

    def sent_all(copy, par, count, at, me):
        @pl.loop(1, count)
        def _(i):
            copy(par, at(i), me).wait_send()

    def sum_begin(par, whole):
        for i in range(nc):
            ga[i] = whole[i * part : (i + 1) * part]
        g1[par, c] = ga[c]
        send_all(gram_1, par, nc, on_row, c)

    def sum_middle(par):
        recv_all(gram_1, par, nc, on_row)
        g2[par, r] = jnp.sum(g1[par], axis=0)
        send_all(gram_2, par, nr, on_col, r)
        sent_all(gram_1, par, nc, on_row, c)

    def sum_late(par):
        recv_all(gram_2, par, nr, on_col)
        g3[par, c] = jnp.sum(g2[par], axis=0)
        send_all(gram_3, par, nc, on_row, c)
        sent_all(gram_2, par, nr, on_col, r)

    def sum_end(par):
        recv_all(gram_3, par, nc, on_row)
        sent_all(gram_3, par, nc, on_row, c)
        return jnp.concatenate([g3[par, i] for i in range(nc)], axis=0)

    begin = start[...]
    gram = mm_nt(begin, begin)
    for k in range(cap):
        vals_t[k] = vals[k].T
    scol[cap] = jnp.zeros(scol.shape[1:], F32)
    srow[cap] = jnp.zeros(srow.shape[1:], F32)
    pl.semaphore_wait(barrier, nr + nc - 2)

    sum_begin(0, jnp.concatenate([gram, gram], axis=1))
    sum_middle(0)
    sum_late(0)
    total = sum_end(0)
    _, inverse = factor(total[:, :width])
    first = mm(inverse, begin)
    q_s[...] = first
    v_s[...] = first
    qp_s[...] = jnp.zeros_like(first)

    def coefficients(total, turn):
        a = total[:, :width]
        g = total[:, width:]
        upper, inverse = factor(g - mm_nt(a, a))
        row = lax.broadcasted_iota(jnp.int32, a.shape, 0)
        lane = lax.broadcasted_iota(jnp.int32, a.shape, 1)
        diag_o[turn] = a + (row == lane).astype(F32)
        off_o[turn] = upper.T
        return a, upper, inverse

    def step(turn, _):
        par = lax.rem(turn, 2)
        later = turn > 0
        narrow = v_s[...].astype(BF)
        xcol[par, r] = narrow
        xrow[par, c] = narrow

        @pl.when(later)
        def _():
            v = v_s[...]
            sum_begin(par, mm_nt(v, jnp.concatenate([q_s[...], v], axis=0)))

        send_all(ag_row, par, nc, on_row, c)
        send_all(ag_col, par, nr, on_col, r)

        @pl.when(later)
        def _():
            sum_middle(par)

        recv_all(ag_row, par, nc, on_row)
        wrow[...] = xrow[par]
        for k in range(cap):
            term = jnp.dot(
                wrow[tab[k]], vals[k], preferred_element_type=F32
            )
            scol[k] = term + scol[tab[2 * cap + k]]
        for i in range(nr):
            pcol[i] = scol[tab[4 * cap + nc + i]].astype(BF)
        rcol[par, r] = pcol[r]
        send_all(rs_col, par, nr, on_col, r)

        recv_all(ag_col, par, nr, on_col)
        wcol[...] = xcol[par]
        for k in range(cap):
            term = jnp.dot(
                wcol[tab[cap + k]], vals_t[k], preferred_element_type=F32
            )
            srow[k] = term + srow[tab[3 * cap + k]]
        for i in range(nc):
            prow[i] = srow[tab[4 * cap + i]].astype(BF)
        rrow[par, c] = prow[c]
        send_all(rs_row, par, nc, on_row, c)

        @pl.when(later)
        def _():
            sum_late(par)
            a, upper, inverse = coefficients(sum_end(par), turn - 1)
            q = q_s[...]
            base = jnp.concatenate(
                [v_s[...] - mm(a, q), mm(a, qs_s[...])], axis=1
            )
            base = mm(inverse, base)
            edge = q.shape[1]
            q_s[...] = base[:, :edge]
            qs_s[...] = base[:, edge:]
            qp_s[...] = mm(upper, q)
            e_s[...] = inverse

        recv_all(rs_row, par, nc, on_row)
        recv_all(rs_col, par, nr, on_col)
        share = jnp.sum(rrow[par].astype(F32), axis=0) + jnp.sum(
            rcol[par].astype(F32), axis=0
        )

        @pl.when(later)
        def _():
            image = mm(e_s[...], share) - qs_s[...]
            qs_s[...] = image
            v_s[...] = -image - qp_s[...]

        @pl.when(jnp.logical_not(later))
        def _():
            qs_s[...] = share
            v_s[...] = -share

        sent_all(ag_row, par, nc, on_row, c)
        sent_all(ag_col, par, nr, on_col, r)
        sent_all(rs_row, par, nc, on_row, c)
        sent_all(rs_col, par, nr, on_col, r)
        return 0

    lax.fori_loop(0, STEPS, step, 0)

    v = v_s[...]
    q = q_s[...]
    sum_begin(0, mm_nt(v, jnp.concatenate([q, v], axis=0)))
    sum_middle(0)
    sum_late(0)
    a, _, inverse = coefficients(sum_end(0), STEPS - 1)
    basis_o[...] = mm(inverse, v - mm(a, q))


def tables(counts, block_rows, block_cols, nr, nc):
    cap = block_rows.shape[0]
    slot = jnp.arange(cap, dtype=jnp.int32)
    every_row = jnp.arange(nc, dtype=jnp.int32)
    every_col = jnp.arange(nr, dtype=jnp.int32)
    live = jnp.broadcast_to(counts, (cap,))

    def latest(keys, wanted, below):
        hit = (keys[None, :] == wanted[:, None]) & (slot[None, :] < below[:, None])
        found = jnp.max(jnp.where(hit, slot[None, :], -1), axis=1)
        return jnp.where(found < 0, cap, found)

    return jnp.concatenate(
        [
            jnp.clip(block_rows, 0, nc - 1),
            jnp.clip(block_cols, 0, nr - 1),
            latest(block_cols, block_cols, slot),
            latest(block_rows, block_rows, slot),
            latest(block_rows, every_row, jnp.broadcast_to(counts, (nc,))),
            latest(block_cols, every_col, jnp.broadcast_to(counts, (nr,))),
        ]
    )


def per_device(counts, block_rows, block_cols, values, start_block):
    nr = lax.axis_size("row")
    nc = lax.axis_size("col")
    tab = tables(counts[0, 0], block_rows[0, 0], block_cols[0, 0], nr, nc)
    vals = values[0, 0]
    cap, edge, _ = vals.shape
    width = start_block.shape[0]
    part = width // nc
    vmem = pl.BlockSpec(memory_space=pltpu.VMEM)
    dma = pltpu.SemaphoreType.DMA

    def block(*lead, dtype=BF):
        return pltpu.VMEM((*lead, width, edge), dtype)

    def piece(*lead):
        return pltpu.VMEM((*lead, part, 2 * width), F32)

    return pl.pallas_call(
        functools.partial(kernel, nr, nc),
        out_shape=(
            jax.ShapeDtypeStruct((STEPS, width, width), F32),
            jax.ShapeDtypeStruct((STEPS, width, width), F32),
            jax.ShapeDtypeStruct((width, edge), F32),
        ),
        in_specs=[pl.BlockSpec(memory_space=pltpu.SMEM), vmem, vmem],
        out_specs=(vmem, vmem, vmem),
        scratch_shapes=[
            pltpu.VMEM((cap, edge, edge), BF),
            block(2, nr),
            block(2, nc),
            block(nr),
            block(nc),
            block(cap + 1, dtype=F32),
            block(cap + 1, dtype=F32),
            block(nr),
            block(nc),
            block(2, nr),
            block(2, nc),
            piece(nc),
            piece(2, nc),
            piece(2, nr),
            piece(2, nc),
            block(dtype=F32),
            block(dtype=F32),
            block(dtype=F32),
            block(dtype=F32),
            pltpu.VMEM((width, width), F32),
            dma((nr,)),
            dma((2, nr)),
            dma((nc,)),
            dma((2, nc)),
            dma((nr,)),
            dma((2, nr)),
            dma((nc,)),
            dma((2, nc)),
            dma((nc,)),
            dma((2, nc)),
            dma((nr,)),
            dma((2, nr)),
            dma((nc,)),
            dma((2, nc)),
        ],
        compiler_params=pltpu.CompilerParams(
            collective_id=0, has_side_effects=True, vmem_limit_bytes=40 << 20
        ),
        name="lanczos",
    )(tab, vals, start_block)


def solution(mesh):
    in_specs = (
        P("row", "col"),
        P("row", "col", None),
        P("row", "col", None),
        P("row", "col", None, None, None),
        P(None, ("row", "col")),
    )
    out_specs = (P(), P(), P(None, ("row", "col")))
    return jax.shard_map(
        per_device, mesh=mesh, in_specs=in_specs, out_specs=out_specs, check_vma=False
    )
```

```python
import functools

import jax
import jax.numpy as jnp
from jax import lax
from jax.experimental import pallas as pl
from jax.experimental.pallas import tpu as pltpu
from jax.sharding import PartitionSpec as P

STEPS = 4
HI = lax.Precision.HIGHEST
F32 = jnp.float32
BF = jnp.bfloat16
MESH = pl.DeviceIdType.MESH


def mm(a, b):
    return lax.dot_general(
        a, b, (((1,), (0,)), ((), ())), precision=HI, preferred_element_type=F32
    )


def mm_nt(a, b):
    return lax.dot_general(
        a, b, (((1,), (1,)), ((), ())), precision=HI, preferred_element_type=F32
    )


GROUP = 8


def factor(gram):
    n = gram.shape[0]
    row = lax.broadcasted_iota(jnp.int32, (n, 2 * n), 0)
    lane = lax.broadcasted_iota(jnp.int32, (n, 2 * n), 1)
    eye = (row[:, :n] == lane[:, :n]).astype(F32)
    m = jnp.concatenate([gram, eye], axis=1)
    above = lax.broadcasted_iota(jnp.int32, (GROUP, 2 * n), 0)
    done = []
    for first in range(0, n, GROUP):
        cols = [
            jnp.broadcast_to(m[:, first + j : first + j + 1], m.shape)
            for j in range(GROUP)
        ]
        for j in range(GROUP):
            inverse = 1.0 / cols[j][j : j + 1]
            head = jnp.where(above > j, cols[j][:GROUP], 0.0)
            mult = head if m.shape[0] == GROUP else jnp.concatenate(
                [head, cols[j][GROUP:]], axis=0
            )
            mult = mult * inverse
            for i in range(j + 1, GROUP):
                cols[i] = cols[i] - mult * cols[i][j : j + 1]
            m = m - mult * m[j : j + 1]
        done.append(m[:GROUP])
        m = m[GROUP:]
    m = jnp.concatenate(done, axis=0)
    diag = jnp.sum(jnp.where(row == lane, m, 0.0), axis=1, keepdims=True)
    m = m / jnp.sqrt(diag)
    upper = jnp.where(lane[:, :n] >= row[:, :n], m[:, :n], 0.0)
    return upper, m[:, n:]


def kernel(
    nr,
    nc,
    counts,
    block_rows,
    block_cols,
    vals_hbm,
    start_hbm,
    diag_o,
    off_o,
    basis_o,
    tab,
    vals,
    start,
    vals_t,
    xcol,
    xrow,
    wcol,
    wrow,
    scol,
    srow,
    pcol,
    psib,
    pown,
    pfin,
    rcol,
    rsib,
    rrow,
    ga,
    g1,
    g2,
    g3,
    q_s,
    qs_s,
    qp_s,
    v_s,
    e_s,
    load_sem,
    ax_send,
    ax_recv,
    ay_send,
    ay_recv,
    bx_send,
    bx_recv,
    bs_send,
    bs_recv,
    by_send,
    by_recv,
    g1_send,
    g1_recv,
    g2_send,
    g2_recv,
    g3_send,
    g3_recv,
):
    cap = vals.shape[0]
    width, edge = start.shape
    part = width // nc
    chips = nc // 2
    r = lax.axis_index("row")
    c = lax.axis_index("col")
    core = lax.rem(c, 2)
    chip = c // 2
    other = chip * 2 + 1 - core

    load_start = pltpu.make_async_copy(start_hbm, start, load_sem.at[0])
    load_vals = pltpu.make_async_copy(vals_hbm, vals, load_sem.at[1])
    load_start.start()
    load_vals.start()

    def on_col(i):
        return lax.rem(r + i, nr)

    def on_row(i):
        return lax.rem(c + i, nc)

    def on_chip(i):
        return lax.rem(chip + i, chips)

    xcol[...] = jnp.zeros_like(xcol)
    rcol[...] = jnp.zeros_like(rcol)

    barrier = pltpu.get_barrier_semaphore()

    @pl.loop(1, nr)
    def _(i):
        pl.semaphore_signal(
            barrier, inc=1, device_id=(on_col(i), c), device_id_type=MESH
        )

    @pl.loop(1, nc)
    def _(i):
        pl.semaphore_signal(
            barrier, inc=1, device_id=(r, on_row(i)), device_id_type=MESH
        )

    def remote(src, dst, send, recv, device):
        return pltpu.make_async_remote_copy(
            src_ref=src,
            dst_ref=dst,
            send_sem=send,
            recv_sem=recv,
            device_id=device,
            device_id_type=MESH,
        )

    def ag_col(par, to, slot):
        return remote(
            xcol.at[par, r],
            xcol.at[par, slot],
            ax_send.at[to],
            ax_recv.at[par, slot],
            (to, c),
        )

    def ag_row(par, to, slot):
        return remote(
            xrow.at[par, slot],
            xrow.at[par, slot],
            ay_send.at[to],
            ay_recv.at[par, slot],
            (r, to),
        )

    def ag_pass(par, at):
        return remote(
            xrow.at[par, at * 2 + core],
            xrow.at[par, at * 2 + core],
            ay_send.at[nc + at],
            ay_recv.at[par, at * 2 + core],
            (r, other),
        )

    def ag_passed(par, at):
        return remote(
            xrow.at[par, at * 2 + 1 - core],
            xrow.at[par, at * 2 + 1 - core],
            ay_send.at[nc + at],
            ay_recv.at[par, at * 2 + 1 - core],
            (r, other),
        )

    def rs_col(par, to, slot):
        return remote(
            pcol.at[to],
            rcol.at[par, slot],
            bx_send.at[to],
            bx_recv.at[par, slot],
            (to, c),
        )

    def rs_sib(par, i):
        return remote(
            psib.at[i],
            rsib.at[par, i],
            bs_send.at[i],
            bs_recv.at[par, i],
            (r, other),
        )

    def rs_row(par, i, to, slot):
        return remote(
            pfin.at[i],
            rrow.at[par, slot],
            by_send.at[i],
            by_recv.at[par, slot],
            (r, to * 2 + core),
        )

    def gram_1(par, to, slot):
        return remote(
            ga.at[to],
            g1.at[par, slot],
            g1_send.at[to],
            g1_recv.at[par, slot],
            (r, to),
        )

    def gram_2(par, to, slot):
        return remote(
            g2.at[par, r],
            g2.at[par, slot],
            g2_send.at[to],
            g2_recv.at[par, slot],
            (to, c),
        )

    def gram_3(par, to, slot):
        return remote(
            g3.at[par, c],
            g3.at[par, slot],
            g3_send.at[to],
            g3_recv.at[par, slot],
            (r, to),
        )

    def send_all(copy, par, count, at, me):
        @pl.loop(1, count)
        def _(i):
            copy(par, at(i), me).start()

    def recv_all(copy, par, count, at):
        @pl.loop(1, count)
        def _(i):
            copy(par, at(i), at(i)).wait_recv()

    def sent_all(copy, par, count, at, me):
        @pl.loop(1, count)
        def _(i):
            copy(par, at(i), me).wait_send()

    def sum_begin(par, whole):
        for i in range(nc):
            ga[i] = whole[i * part : (i + 1) * part]
        g1[par, c] = ga[c]
        send_all(gram_1, par, nc, on_row, c)

    def sum_middle(par):
        recv_all(gram_1, par, nc, on_row)
        g2[par, r] = jnp.sum(g1[par], axis=0)
        send_all(gram_2, par, nr, on_col, r)
        sent_all(gram_1, par, nc, on_row, c)

    def sum_late(par):
        recv_all(gram_2, par, nr, on_col)
        g3[par, c] = jnp.sum(g2[par], axis=0)
        send_all(gram_3, par, nc, on_row, c)
        sent_all(gram_2, par, nr, on_col, r)

    def sum_end(par):
        recv_all(gram_3, par, nc, on_row)
        sent_all(gram_3, par, nc, on_row, c)
        return jnp.concatenate([g3[par, i] for i in range(nc)], axis=0)

    at_prev_row, at_prev_col = 0, cap
    at_last_row = 2 * cap
    at_last_col = 2 * cap + nc
    live = counts[0]

    def latest(keys, want, below):
        found = jnp.int32(cap)
        for k in range(cap):
            hit = (keys[k] == want) & (k < below)
            found = jnp.where(hit, k, found)
        return found

    @pl.loop(0, cap)
    def _(k):
        tab[at_prev_row + k] = latest(block_rows, block_rows[k], k)
        tab[at_prev_col + k] = latest(block_cols, block_cols[k], k)

    @pl.loop(0, nc)
    def _(i):
        tab[at_last_row + i] = latest(block_rows, i, live)

    @pl.loop(0, nr)
    def _(i):
        tab[at_last_col + i] = latest(block_cols, i, live)

    load_start.wait()
    begin = start[...]
    gram = mm_nt(begin, begin)
    scol[cap] = jnp.zeros(scol.shape[1:], F32)
    srow[cap] = jnp.zeros(srow.shape[1:], F32)
    pl.semaphore_wait(barrier, nr + nc - 2)

    sum_begin(0, jnp.concatenate([gram, gram], axis=1))
    load_vals.wait()
    for k in range(cap):
        vals_t[k] = vals[k].T
    sum_middle(0)
    sum_late(0)
    total = sum_end(0)
    _, inverse = factor(total[:, :width])
    first = mm(inverse, begin)
    q_s[...] = first
    v_s[...] = first
    qp_s[...] = jnp.zeros_like(first)

    def coefficients(total, turn):
        a = total[:, :width]
        g = total[:, width:]
        upper, inverse = factor(g - mm_nt(a, a))
        row = lax.broadcasted_iota(jnp.int32, a.shape, 0)
        lane = lax.broadcasted_iota(jnp.int32, a.shape, 1)
        diag_o[turn] = a + (row == lane).astype(F32)
        off_o[turn] = upper.T
        return a, upper, inverse

    def step(turn, _):
        par = lax.rem(turn, 2)
        later = turn > 0
        narrow = v_s[...].astype(BF)
        xrow[par, c] = narrow
        xcol[par, r] = narrow

        @pl.loop(1, chips)
        def _(i):
            ag_row(par, on_chip(i) * 2 + core, c).start()

        ag_pass(par, chip).start()

        @pl.loop(0, r)
        def _(to):
            ag_col(par, to, r).start()

        @pl.when(later)
        def _():
            v = v_s[...]
            sum_begin(par, mm_nt(v, jnp.concatenate([q_s[...], v], axis=0)))

        @pl.loop(1, chips)
        def _(i):
            at = on_chip(i)
            ag_row(par, at * 2 + core, at * 2 + core).wait_recv()
            ag_pass(par, at).start()

        @pl.when(later)
        def _():
            sum_middle(par)

        @pl.loop(0, chips)
        def _(i):
            ag_passed(par, on_chip(i)).wait_recv()

        wrow[...] = xrow[par]
        for k in range(cap):
            term = jnp.dot(
                wrow[block_rows[k]], vals[k], preferred_element_type=F32
            )
            scol[k] = term + scol[tab[at_prev_col + k]]
        for i in range(nr):
            pcol[i] = scol[tab[at_last_col + i]].astype(BF)
        rcol[par, r] = pcol[r]

        @pl.loop(0, nr - 1 - r)
        def _(i):
            rs_col(par, nr - 1 - i, r).start()

        @pl.when(later)
        def _():
            sum_late(par)

        @pl.loop(r + 1, nr)
        def _(i):
            ag_col(par, i, i).wait_recv()

        wcol[...] = xcol[par]
        for k in range(cap):
            term = jnp.dot(
                wcol[block_cols[k]], vals_t[k], preferred_element_type=F32
            )
            srow[k] = term + srow[tab[at_prev_row + k]]
        for i in range(chips):
            at = at_last_row + on_chip(i + 1) * 2
            psib[i] = srow[tab[at + 1 - core]].astype(BF)
            pown[i] = srow[tab[at + core]]
            rs_sib(par, i).start()
        for i in range(chips):
            rs_sib(par, i).wait_recv()
            both = pown[i] + rsib[par, i].astype(F32)
            if i < chips - 1:
                pfin[i] = both.astype(BF)
                rs_row(par, i, on_chip(i + 1), chip).start()
            else:
                rrow[par, chip] = both.astype(BF)

        @pl.when(later)
        def _():
            a, upper, inverse = coefficients(sum_end(par), turn - 1)
            q = q_s[...]
            base = jnp.concatenate(
                [v_s[...] - mm(a, q), mm(a, qs_s[...])], axis=1
            )
            base = mm(inverse, base)
            q_s[...] = base[:, :edge]
            qs_s[...] = base[:, edge:]
            qp_s[...] = mm(upper, q)
            e_s[...] = inverse

        @pl.loop(0, chips - 1)
        def _(i):
            rs_row(par, i, on_chip(i + 1), on_chip(i + 1)).wait_recv()

        @pl.loop(0, r)
        def _(i):
            rs_col(par, i, i).wait_recv()

        share = jnp.sum(rrow[par].astype(F32), axis=0) + jnp.sum(
            rcol[par].astype(F32), axis=0
        )

        @pl.when(later)
        def _():
            image = mm(e_s[...], share) - qs_s[...]
            qs_s[...] = image
            v_s[...] = -image - qp_s[...]

        @pl.when(jnp.logical_not(later))
        def _():
            qs_s[...] = share
            v_s[...] = -share

        @pl.loop(1, chips)
        def _(i):
            ag_row(par, on_chip(i) * 2 + core, c).wait_send()

        @pl.loop(0, chips)
        def _(i):
            ag_pass(par, i).wait_send()
            rs_sib(par, i).wait_send()

        @pl.loop(0, chips - 1)
        def _(i):
            rs_row(par, i, on_chip(i + 1), chip).wait_send()

        @pl.loop(0, r)
        def _(to):
            ag_col(par, to, r).wait_send()

        @pl.loop(0, nr - 1 - r)
        def _(i):
            rs_col(par, nr - 1 - i, r).wait_send()

        return 0

    lax.fori_loop(0, STEPS, step, 0)

    v = v_s[...]
    q = q_s[...]
    sum_begin(0, mm_nt(v, jnp.concatenate([q, v], axis=0)))
    sum_middle(0)
    sum_late(0)
    a, _, inverse = coefficients(sum_end(0), STEPS - 1)
    basis_o[...] = mm(inverse, v - mm(a, q))


def per_device(counts, block_rows, block_cols, values, start_block):
    nr = lax.axis_size("row")
    nc = lax.axis_size("col")
    cap, edge, _ = values.shape[2:]
    width = start_block.shape[0]
    part = width // nc
    chips = nc // 2
    smem = pl.BlockSpec(memory_space=pltpu.SMEM)
    vmem = pl.BlockSpec(memory_space=pltpu.VMEM)
    anywhere = pl.BlockSpec(memory_space=pl.ANY)
    dma = pltpu.SemaphoreType.DMA

    def block(*lead, dtype=BF):
        return pltpu.VMEM((*lead, width, edge), dtype)

    def piece(*lead):
        return pltpu.VMEM((*lead, part, 2 * width), F32)

    return pl.pallas_call(
        functools.partial(kernel, nr, nc),
        out_shape=(
            jax.ShapeDtypeStruct((STEPS, width, width), F32),
            jax.ShapeDtypeStruct((STEPS, width, width), F32),
            jax.ShapeDtypeStruct((width, edge), F32),
        ),
        in_specs=[smem, smem, smem, anywhere, anywhere],
        out_specs=(vmem, vmem, vmem),
        scratch_shapes=[
            pltpu.SMEM((2 * cap + nc + nr,), jnp.int32),
            pltpu.VMEM((cap, edge, edge), BF),
            block(dtype=F32),
            pltpu.VMEM((cap, edge, edge), BF),
            block(2, nr),
            block(2, nc),
            block(nr),
            block(nc),
            block(cap + 1, dtype=F32),
            block(cap + 1, dtype=F32),
            block(nr),
            block(chips),
            block(chips, dtype=F32),
            block(chips),
            block(2, nr),
            block(2, chips),
            block(2, chips),
            piece(nc),
            piece(2, nc),
            piece(2, nr),
            piece(2, nc),
            block(dtype=F32),
            block(dtype=F32),
            block(dtype=F32),
            block(dtype=F32),
            pltpu.VMEM((width, width), F32),
            dma((2,)),
            dma((nr,)),
            dma((2, nr)),
            dma((nc + chips,)),
            dma((2, nc)),
            dma((nr,)),
            dma((2, nr)),
            dma((chips,)),
            dma((2, chips)),
            dma((chips,)),
            dma((2, chips)),
            dma((nc,)),
            dma((2, nc)),
            dma((nr,)),
            dma((2, nr)),
            dma((nc,)),
            dma((2, nc)),
        ],
        compiler_params=pltpu.CompilerParams(
            collective_id=0, has_side_effects=True, vmem_limit_bytes=40 << 20
        ),
        name="lanczos",
    )(counts[0], block_rows[0, 0], block_cols[0, 0], values[0, 0], start_block)


def solution(mesh):
    in_specs = (
        P("row", "col"),
        P("row", "col", None),
        P("row", "col", None),
        P("row", "col", None, None, None),
        P(None, ("row", "col")),
    )
    out_specs = (P(), P(), P(None, ("row", "col")))
    return jax.shard_map(
        per_device, mesh=mesh, in_specs=in_specs, out_specs=out_specs, check_vma=False
    )
```

```python
import functools

import jax
import jax.numpy as jnp
from jax import lax
from jax.experimental import pallas as pl
from jax.experimental.pallas import tpu as pltpu
from jax.sharding import PartitionSpec as P

STEPS = 4
HI = lax.Precision.HIGHEST
F32 = jnp.float32
BF = jnp.bfloat16
MESH = pl.DeviceIdType.MESH


def mm(a, b):
    return lax.dot_general(
        a, b, (((1,), (0,)), ((), ())), precision=HI, preferred_element_type=F32
    )


def mm_nt(a, b):
    return lax.dot_general(
        a, b, (((1,), (1,)), ((), ())), precision=HI, preferred_element_type=F32
    )


GROUP = 8


def factor(gram):
    n = gram.shape[0]
    row = lax.broadcasted_iota(jnp.int32, (n, 2 * n), 0)
    lane = lax.broadcasted_iota(jnp.int32, (n, 2 * n), 1)
    eye = (row[:, :n] == lane[:, :n]).astype(F32)
    m = jnp.concatenate([gram, eye], axis=1)
    above = lax.broadcasted_iota(jnp.int32, (GROUP, 2 * n), 0)
    done = []
    for first in range(0, n, GROUP):
        cols = [
            jnp.broadcast_to(m[:, first + j : first + j + 1], m.shape)
            for j in range(GROUP)
        ]
        for j in range(GROUP):
            inverse = 1.0 / cols[j][j : j + 1]
            head = jnp.where(above > j, cols[j][:GROUP], 0.0)
            mult = head if m.shape[0] == GROUP else jnp.concatenate(
                [head, cols[j][GROUP:]], axis=0
            )
            mult = mult * inverse
            for i in range(j + 1, GROUP):
                cols[i] = cols[i] - mult * cols[i][j : j + 1]
            m = m - mult * m[j : j + 1]
        done.append(m[:GROUP])
        m = m[GROUP:]
    m = jnp.concatenate(done, axis=0)
    diag = jnp.sum(jnp.where(row == lane, m, 0.0), axis=1, keepdims=True)
    m = m / jnp.sqrt(diag)
    upper = jnp.where(lane[:, :n] >= row[:, :n], m[:, :n], 0.0)
    return upper, m[:, n:]


def kernel(
    nr,
    nc,
    counts_hbm,
    rows_hbm,
    cols_hbm,
    vals_hbm,
    start_hbm,
    diag_o,
    off_o,
    basis_o,
    counts,
    rows,
    cols,
    tab,
    vals,
    start,
    vals_t,
    xcol,
    xrow,
    wcol,
    wrow,
    scol,
    srow,
    pcol,
    psib,
    pown,
    pfin,
    rcol,
    rsib,
    rrow,
    ga,
    g1,
    g2,
    g3,
    q_s,
    qs_s,
    qp_s,
    v_s,
    e_s,
    load_sem,
    ax_send,
    ax_recv,
    ay_send,
    ay_recv,
    bx_send,
    bx_recv,
    bs_send,
    bs_recv,
    by_send,
    by_recv,
    g1_send,
    g1_recv,
    g2_send,
    g2_recv,
    g3_send,
    g3_recv,
):
    cap = vals.shape[0]
    width, edge = start.shape
    part = width // nc
    chips = nc // 2
    r = lax.axis_index("row")
    c = lax.axis_index("col")
    core = lax.rem(c, 2)
    chip = c // 2
    other = chip * 2 + 1 - core

    load_start = pltpu.make_async_copy(start_hbm, start, load_sem.at[0])
    load_vals = pltpu.make_async_copy(vals_hbm.at[0, 0], vals, load_sem.at[1])
    load_scalars = [
        pltpu.make_async_copy(src, dst, load_sem.at[2 + i])
        for i, (src, dst) in enumerate(
            ((counts_hbm, counts), (rows_hbm, rows), (cols_hbm, cols))
        )
    ]
    load_start.start()
    for load in load_scalars:
        load.start()
    load_vals.start()

    def on_col(i):
        return lax.rem(r + i, nr)

    def on_row(i):
        return lax.rem(c + i, nc)

    def on_chip(i):
        return lax.rem(chip + i, chips)

    xcol[...] = jnp.zeros_like(xcol)
    rcol[...] = jnp.zeros_like(rcol)

    barrier = pltpu.get_barrier_semaphore()

    @pl.loop(1, nr)
    def _(i):
        pl.semaphore_signal(
            barrier, inc=1, device_id=(on_col(i), c), device_id_type=MESH
        )

    @pl.loop(1, nc)
    def _(i):
        pl.semaphore_signal(
            barrier, inc=1, device_id=(r, on_row(i)), device_id_type=MESH
        )

    def remote(src, dst, send, recv, device):
        return pltpu.make_async_remote_copy(
            src_ref=src,
            dst_ref=dst,
            send_sem=send,
            recv_sem=recv,
            device_id=device,
            device_id_type=MESH,
        )

    def ag_col(par, to, slot):
        return remote(
            xcol.at[par, r],
            xcol.at[par, slot],
            ax_send.at[to],
            ax_recv.at[par, slot],
            (to, c),
        )

    def ag_row(par, to, slot):
        return remote(
            xrow.at[par, slot],
            xrow.at[par, slot],
            ay_send.at[to],
            ay_recv.at[par, slot],
            (r, to),
        )

    def ag_pass(par, at):
        return remote(
            xrow.at[par, at * 2 + core],
            xrow.at[par, at * 2 + core],
            ay_send.at[nc + at],
            ay_recv.at[par, at * 2 + core],
            (r, other),
        )

    def ag_passed(par, at):
        return remote(
            xrow.at[par, at * 2 + 1 - core],
            xrow.at[par, at * 2 + 1 - core],
            ay_send.at[nc + at],
            ay_recv.at[par, at * 2 + 1 - core],
            (r, other),
        )

    def rs_col(par, to, slot):
        return remote(
            pcol.at[to],
            rcol.at[par, slot],
            bx_send.at[to],
            bx_recv.at[par, slot],
            (to, c),
        )

    def rs_sib(par, i):
        return remote(
            psib.at[i],
            rsib.at[par, i],
            bs_send.at[i],
            bs_recv.at[par, i],
            (r, other),
        )

    def rs_row(par, i, to, slot):
        return remote(
            pfin.at[i],
            rrow.at[par, slot],
            by_send.at[i],
            by_recv.at[par, slot],
            (r, to * 2 + core),
        )

    def gram_1(par, to, slot):
        return remote(
            ga.at[to],
            g1.at[par, slot],
            g1_send.at[to],
            g1_recv.at[par, slot],
            (r, to),
        )

    def gram_2(par, to, slot):
        return remote(
            g2.at[par, r],
            g2.at[par, slot],
            g2_send.at[to],
            g2_recv.at[par, slot],
            (to, c),
        )

    def gram_3(par, to, slot):
        return remote(
            g3.at[par, c],
            g3.at[par, slot],
            g3_send.at[to],
            g3_recv.at[par, slot],
            (r, to),
        )

    nx = min(4, chips)
    ny = chips // nx
    y, x = chip // nx, lax.rem(chip, nx)

    def ring(d, n):
        return min(d, n - d)

    plane = sorted(
        (
            (dy, dx, dc)
            for dy in range(ny)
            for dx in range(nx)
            for dc in range(2)
            if (dy, dx, dc) != (0, 0, 0)
        ),
        key=lambda o: -(10 * (ring(o[0], ny) + ring(o[1], nx)) + o[2]),
    )
    far_row = []
    for dy, dx, dc in plane:
        at = lax.rem(y + dy, ny) * nx + lax.rem(x + dx, nx)
        far_row.append(at * 2 + (core if dc == 0 else 1 - core))
    far_chip = [at for dy, dx, dc in plane if dc == 0 for at in (
        lax.rem(y + dy, ny) * nx + lax.rem(x + dx, nx),)]
    far_col = [on_col(d) for d in sorted(range(1, nr), key=lambda d: -ring(d, nr))]

    def send_all(copy, par, peers, me):
        for to in peers:
            copy(par, to, me).start()

    def recv_all(copy, par, peers):
        for to in reversed(peers):
            copy(par, to, to).wait_recv()

    def sent_all(copy, par, peers, me):
        for to in peers:
            copy(par, to, me).wait_send()

    def sum_begin(par, whole):
        for i in range(nc):
            ga[i] = whole[i * part : (i + 1) * part]
        g1[par, c] = ga[c]
        send_all(gram_1, par, far_row, c)

    def sum_middle(par):
        recv_all(gram_1, par, far_row)
        g2[par, r] = jnp.sum(g1[par], axis=0)
        send_all(gram_2, par, far_col, r)
        sent_all(gram_1, par, far_row, c)

    def sum_late(par):
        recv_all(gram_2, par, far_col)
        g3[par, c] = jnp.sum(g2[par], axis=0)
        send_all(gram_3, par, far_row, c)
        sent_all(gram_2, par, far_col, r)

    def sum_end(par):
        recv_all(gram_3, par, far_row)
        sent_all(gram_3, par, far_row, c)
        return jnp.concatenate([g3[par, i] for i in range(nc)], axis=0)

    at_prev_row, at_prev_col = 0, cap
    at_last_row = 2 * cap
    at_last_col = 2 * cap + nc
    for load in load_scalars:
        load.wait()
    live = counts[0, 0]

    def latest(keys, want, below):
        found = jnp.int32(cap)
        for k in range(cap):
            hit = (keys[0, 0, k] == want) & (k < below)
            found = jnp.where(hit, k, found)
        return found

    @pl.loop(0, cap)
    def _(k):
        tab[at_prev_row + k] = latest(rows, rows[0, 0, k], k)
        tab[at_prev_col + k] = latest(cols, cols[0, 0, k], k)

    @pl.loop(0, nc)
    def _(i):
        tab[at_last_row + i] = latest(rows, i, live)

    @pl.loop(0, nr)
    def _(i):
        tab[at_last_col + i] = latest(cols, i, live)

    load_start.wait()
    begin = start[...]
    gram = mm_nt(begin, begin)
    scol[cap] = jnp.zeros(scol.shape[1:], F32)
    srow[cap] = jnp.zeros(srow.shape[1:], F32)
    pl.semaphore_wait(barrier, nr + nc - 2)

    sum_begin(0, jnp.concatenate([gram, gram], axis=1))
    load_vals.wait()
    for k in range(cap):
        vals_t[k] = vals[k].T
    sum_middle(0)
    sum_late(0)
    total = sum_end(0)
    _, inverse = factor(total[:, :width])
    first = mm(inverse, begin)
    q_s[...] = first
    v_s[...] = first
    qp_s[...] = jnp.zeros_like(first)

    def coefficients(total, turn):
        a = total[:, :width]
        g = total[:, width:]
        upper, inverse = factor(g - mm_nt(a, a))
        row = lax.broadcasted_iota(jnp.int32, a.shape, 0)
        lane = lax.broadcasted_iota(jnp.int32, a.shape, 1)
        diag_o[turn] = a + (row == lane).astype(F32)
        off_o[turn] = upper.T
        return a, upper, inverse

    def step(turn, _):
        par = lax.rem(turn, 2)
        later = turn > 0
        narrow = v_s[...].astype(BF)
        xrow[par, c] = narrow
        xcol[par, r] = narrow

        @pl.when(later)
        def _():
            v = v_s[...]
            sum_begin(par, mm_nt(v, jnp.concatenate([q_s[...], v], axis=0)))

        for at in far_chip:
            ag_row(par, at * 2 + core, c).start()

        ag_pass(par, chip).start()

        @pl.loop(0, r)
        def _(to):
            ag_col(par, to, r).start()

        @pl.when(later)
        def _():
            sum_middle(par)

        for at in reversed(far_chip):
            ag_row(par, at * 2 + core, at * 2 + core).wait_recv()
            ag_pass(par, at).start()

        @pl.loop(0, chips)
        def _(i):
            ag_passed(par, on_chip(i)).wait_recv()

        wrow[...] = xrow[par]
        for k in range(cap):
            term = jnp.dot(
                wrow[rows[0, 0, k]], vals[k], preferred_element_type=F32
            )
            scol[k] = term + scol[tab[at_prev_col + k]]
        for i in range(nr):
            pcol[i] = scol[tab[at_last_col + i]].astype(BF)
        rcol[par, r] = pcol[r]

        @pl.loop(0, nr - 1 - r)
        def _(i):
            rs_col(par, nr - 1 - i, r).start()

        @pl.loop(r + 1, nr)
        def _(i):
            ag_col(par, i, i).wait_recv()

        wcol[...] = xcol[par]
        for k in range(cap):
            term = jnp.dot(
                wcol[cols[0, 0, k]], vals_t[k], preferred_element_type=F32
            )
            srow[k] = term + srow[tab[at_prev_row + k]]
        for i in range(chips):
            at = at_last_row + on_chip(i + 1) * 2
            psib[i] = srow[tab[at + 1 - core]].astype(BF)
            pown[i] = srow[tab[at + core]]
            rs_sib(par, i).start()

        @pl.when(later)
        def _():
            sum_late(par)

        for i in range(chips):
            rs_sib(par, i).wait_recv()
            both = pown[i] + rsib[par, i].astype(F32)
            if i < chips - 1:
                pfin[i] = both.astype(BF)
                rs_row(par, i, on_chip(i + 1), chip).start()
            else:
                rrow[par, chip] = both.astype(BF)

        @pl.when(later)
        def _():
            a, upper, inverse = coefficients(sum_end(par), turn - 1)
            q = q_s[...]
            q_s[...] = v_s[...] - mm(a, q)
            qs_s[...] = mm(a, qs_s[...])
            qp_s[...] = mm(upper, q)
            e_s[...] = inverse

        @pl.loop(0, chips - 1)
        def _(i):
            rs_row(par, i, on_chip(i + 1), on_chip(i + 1)).wait_recv()

        @pl.loop(0, r)
        def _(i):
            rs_col(par, i, i).wait_recv()

        share = jnp.sum(rrow[par].astype(F32), axis=0) + jnp.sum(
            rcol[par].astype(F32), axis=0
        )

        @pl.when(later)
        def _():
            both = jnp.concatenate([share - qs_s[...], q_s[...]], axis=1)
            both = mm(e_s[...], both)
            image = both[:, :edge]
            qs_s[...] = image
            v_s[...] = -image - qp_s[...]
            q_s[...] = both[:, edge:]

        @pl.when(jnp.logical_not(later))
        def _():
            qs_s[...] = share
            v_s[...] = -share

        @pl.loop(1, chips)
        def _(i):
            ag_row(par, on_chip(i) * 2 + core, c).wait_send()

        @pl.loop(0, chips)
        def _(i):
            ag_pass(par, i).wait_send()
            rs_sib(par, i).wait_send()

        @pl.loop(0, chips - 1)
        def _(i):
            rs_row(par, i, on_chip(i + 1), chip).wait_send()

        @pl.loop(0, r)
        def _(to):
            ag_col(par, to, r).wait_send()

        @pl.loop(0, nr - 1 - r)
        def _(i):
            rs_col(par, nr - 1 - i, r).wait_send()

        return 0

    lax.fori_loop(0, STEPS, step, 0)

    v = v_s[...]
    q = q_s[...]
    sum_begin(0, mm_nt(v, jnp.concatenate([q, v], axis=0)))
    sum_middle(0)
    sum_late(0)
    a, _, inverse = coefficients(sum_end(0), STEPS - 1)
    basis_o[...] = mm(inverse, v - mm(a, q))


def per_device(counts, block_rows, block_cols, values, start_block):
    nr = lax.axis_size("row")
    nc = lax.axis_size("col")
    cap, edge, _ = values.shape[2:]
    width = start_block.shape[0]
    part = width // nc
    chips = nc // 2
    vmem = pl.BlockSpec(memory_space=pltpu.VMEM)
    hbm = pl.BlockSpec(memory_space=pltpu.HBM)
    dma = pltpu.SemaphoreType.DMA

    def block(*lead, dtype=BF):
        return pltpu.VMEM((*lead, width, edge), dtype)

    def piece(*lead):
        return pltpu.VMEM((*lead, part, 2 * width), F32)

    return pl.pallas_call(
        functools.partial(kernel, nr, nc),
        out_shape=(
            jax.ShapeDtypeStruct((STEPS, width, width), F32),
            jax.ShapeDtypeStruct((STEPS, width, width), F32),
            jax.ShapeDtypeStruct((width, edge), F32),
        ),
        in_specs=[hbm] * 5,
        out_specs=(vmem, vmem, vmem),
        scratch_shapes=[
            pltpu.SMEM(counts.shape, jnp.int32),
            pltpu.SMEM(block_rows.shape, jnp.int32),
            pltpu.SMEM(block_cols.shape, jnp.int32),
            pltpu.SMEM((2 * cap + nc + nr,), jnp.int32),
            pltpu.VMEM((cap, edge, edge), BF),
            block(dtype=F32),
            pltpu.VMEM((cap, edge, edge), BF),
            block(2, nr),
            block(2, nc),
            block(nr),
            block(nc),
            block(cap + 1, dtype=F32),
            block(cap + 1, dtype=F32),
            block(nr),
            block(chips),
            block(chips, dtype=F32),
            block(chips),
            block(2, nr),
            block(2, chips),
            block(2, chips),
            piece(nc),
            piece(2, nc),
            piece(2, nr),
            piece(2, nc),
            block(dtype=F32),
            block(dtype=F32),
            block(dtype=F32),
            block(dtype=F32),
            pltpu.VMEM((width, width), F32),
            dma((5,)),
            dma((nr,)),
            dma((2, nr)),
            dma((nc + chips,)),
            dma((2, nc)),
            dma((nr,)),
            dma((2, nr)),
            dma((chips,)),
            dma((2, chips)),
            dma((chips,)),
            dma((2, chips)),
            dma((nc,)),
            dma((2, nc)),
            dma((nr,)),
            dma((2, nr)),
            dma((nc,)),
            dma((2, nc)),
        ],
        compiler_params=pltpu.CompilerParams(
            collective_id=0, has_side_effects=True, vmem_limit_bytes=60 << 20
        ),
        name="lanczos",
    )(counts, block_rows, block_cols, values, start_block)


def solution(mesh):
    in_specs = (
        P("row", "col"),
        P("row", "col", None),
        P("row", "col", None),
        P("row", "col", None, None, None),
        P(None, ("row", "col")),
    )
    out_specs = (P(), P(), P(None, ("row", "col")))
    return jax.shard_map(
        per_device, mesh=mesh, in_specs=in_specs, out_specs=out_specs, check_vma=False
    )
```

```python
import functools

import jax
import jax.numpy as jnp
from jax import lax
from jax.experimental import pallas as pl
from jax.experimental.pallas import tpu as pltpu
from jax.sharding import PartitionSpec as P

STEPS = 4
HI = lax.Precision.HIGHEST
F32 = jnp.float32
BF = jnp.bfloat16
MESH = pl.DeviceIdType.MESH


def mm(a, b):
    return lax.dot_general(
        a, b, (((1,), (0,)), ((), ())), precision=HI, preferred_element_type=F32
    )


def mm_nt(a, b):
    return lax.dot_general(
        a, b, (((1,), (1,)), ((), ())), precision=HI, preferred_element_type=F32
    )


GROUP = 8


def factor(gram):
    n = gram.shape[0]
    row = lax.broadcasted_iota(jnp.int32, (n, 2 * n), 0)
    lane = lax.broadcasted_iota(jnp.int32, (n, 2 * n), 1)
    eye = (row[:, :n] == lane[:, :n]).astype(F32)
    m = jnp.concatenate([gram, eye], axis=1)
    above = lax.broadcasted_iota(jnp.int32, (GROUP, 2 * n), 0)
    done = []
    for first in range(0, n, GROUP):
        cols = [
            jnp.broadcast_to(m[:, first + j : first + j + 1], m.shape)
            for j in range(GROUP)
        ]
        for j in range(GROUP):
            inverse = 1.0 / cols[j][j : j + 1]
            head = jnp.where(above > j, cols[j][:GROUP], 0.0)
            mult = head if m.shape[0] == GROUP else jnp.concatenate(
                [head, cols[j][GROUP:]], axis=0
            )
            mult = mult * inverse
            for i in range(j + 1, GROUP):
                cols[i] = cols[i] - mult * cols[i][j : j + 1]
            m = m - mult * m[j : j + 1]
        done.append(m[:GROUP])
        m = m[GROUP:]
    m = jnp.concatenate(done, axis=0)
    diag = jnp.sum(jnp.where(row == lane, m, 0.0), axis=1, keepdims=True)
    m = m / jnp.sqrt(diag)
    upper = jnp.where(lane[:, :n] >= row[:, :n], m[:, :n], 0.0)
    return upper, m[:, n:]


def kernel(
    eager,
    nr,
    nc,
    counts_hbm,
    rows_hbm,
    cols_hbm,
    vals_hbm,
    start_hbm,
    diag_o,
    off_o,
    basis_o,
    gain_o,
    counts,
    rows,
    cols,
    tab,
    vals,
    start,
    vals_t,
    xcol,
    xrow,
    wcol,
    wrow,
    scol,
    srow,
    pcol,
    psib,
    pown,
    pfin,
    rcol,
    rsib,
    rrow,
    ga,
    g1,
    g2,
    g3,
    q_s,
    qs_s,
    qp_s,
    v_s,
    e_s,
    gain_s,
    load_sem,
    ax_send,
    ax_recv,
    ay_send,
    ay_recv,
    bx_send,
    bx_recv,
    bs_send,
    bs_recv,
    by_send,
    by_recv,
    g1_send,
    g1_recv,
    g2_send,
    g2_recv,
    g3_send,
    g3_recv,
):
    cap = vals.shape[0]
    width, edge = start.shape
    part = width // nc
    chips = nc // 2
    r = lax.axis_index("row")
    c = lax.axis_index("col")
    core = lax.rem(c, 2)
    chip = c // 2
    other = chip * 2 + 1 - core

    load_start = pltpu.make_async_copy(start_hbm, start, load_sem.at[0])
    load_vals = pltpu.make_async_copy(vals_hbm.at[0, 0], vals, load_sem.at[1])
    load_scalars = [
        pltpu.make_async_copy(src, dst, load_sem.at[2 + i])
        for i, (src, dst) in enumerate(
            ((counts_hbm, counts), (rows_hbm, rows), (cols_hbm, cols))
        )
    ]
    load_start.start()
    for load in load_scalars:
        load.start()
    load_vals.start()

    def on_col(i):
        return lax.rem(r + i, nr)

    def on_row(i):
        return lax.rem(c + i, nc)

    def on_chip(i):
        return lax.rem(chip + i, chips)

    xcol[...] = jnp.zeros_like(xcol)
    rcol[...] = jnp.zeros_like(rcol)

    barrier = pltpu.get_barrier_semaphore()

    @pl.loop(1, nr)
    def _(i):
        pl.semaphore_signal(
            barrier, inc=1, device_id=(on_col(i), c), device_id_type=MESH
        )

    @pl.loop(1, nc)
    def _(i):
        pl.semaphore_signal(
            barrier, inc=1, device_id=(r, on_row(i)), device_id_type=MESH
        )

    def remote(src, dst, send, recv, device):
        return pltpu.make_async_remote_copy(
            src_ref=src,
            dst_ref=dst,
            send_sem=send,
            recv_sem=recv,
            device_id=device,
            device_id_type=MESH,
        )

    def ag_col(par, to, slot):
        return remote(
            xcol.at[par, r],
            xcol.at[par, slot],
            ax_send.at[to],
            ax_recv.at[par, slot],
            (to, c),
        )

    def ag_row(par, to, slot):
        return remote(
            xrow.at[par, slot],
            xrow.at[par, slot],
            ay_send.at[to],
            ay_recv.at[par, slot],
            (r, to),
        )

    def ag_pass(par, at):
        return remote(
            xrow.at[par, at * 2 + core],
            xrow.at[par, at * 2 + core],
            ay_send.at[nc + at],
            ay_recv.at[par, at * 2 + core],
            (r, other),
        )

    def ag_passed(par, at):
        return remote(
            xrow.at[par, at * 2 + 1 - core],
            xrow.at[par, at * 2 + 1 - core],
            ay_send.at[nc + at],
            ay_recv.at[par, at * 2 + 1 - core],
            (r, other),
        )

    def rs_col(par, to, slot):
        return remote(
            pcol.at[to],
            rcol.at[par, slot],
            bx_send.at[to],
            bx_recv.at[par, slot],
            (to, c),
        )

    def rs_sib(par, i):
        return remote(
            psib.at[i],
            rsib.at[par, i],
            bs_send.at[i],
            bs_recv.at[par, i],
            (r, other),
        )

    def rs_row(par, i, to, slot):
        return remote(
            pfin.at[i],
            rrow.at[par, slot],
            by_send.at[i],
            by_recv.at[par, slot],
            (r, to * 2 + core),
        )

    def gram_1(par, to, slot):
        return remote(
            ga.at[to],
            g1.at[par, slot],
            g1_send.at[to],
            g1_recv.at[par, slot],
            (r, to),
        )

    def gram_2(par, to, slot):
        return remote(
            g2.at[par, r],
            g2.at[par, slot],
            g2_send.at[to],
            g2_recv.at[par, slot],
            (to, c),
        )

    def gram_3(par, to, slot):
        return remote(
            g3.at[par, c],
            g3.at[par, slot],
            g3_send.at[to],
            g3_recv.at[par, slot],
            (r, to),
        )

    nx = min(4, chips)
    ny = chips // nx
    y, x = chip // nx, lax.rem(chip, nx)

    def ring(d, n):
        return min(d, n - d)

    plane = sorted(
        (
            (dy, dx, dc)
            for dy in range(ny)
            for dx in range(nx)
            for dc in range(2)
            if (dy, dx, dc) != (0, 0, 0)
        ),
        key=lambda o: -(10 * (ring(o[0], ny) + ring(o[1], nx)) + o[2]),
    )
    far_row = []
    for dy, dx, dc in plane:
        at = lax.rem(y + dy, ny) * nx + lax.rem(x + dx, nx)
        far_row.append(at * 2 + (core if dc == 0 else 1 - core))
    far_chip = [at for dy, dx, dc in plane if dc == 0 for at in (
        lax.rem(y + dy, ny) * nx + lax.rem(x + dx, nx),)]
    far_col = [on_col(d) for d in sorted(range(1, nr), key=lambda d: -ring(d, nr))]

    def send_all(copy, par, peers, me):
        for to in peers:
            copy(par, to, me).start()

    def recv_all(copy, par, peers):
        for to in reversed(peers):
            copy(par, to, to).wait_recv()

    def sent_all(copy, par, peers, me):
        for to in peers:
            copy(par, to, me).wait_send()

    def sum_begin(par, whole):
        for i in range(nc):
            ga[i] = whole[i * part : (i + 1) * part]
        g1[par, c] = ga[c]
        send_all(gram_1, par, far_row, c)

    def sum_middle(par):
        recv_all(gram_1, par, far_row)
        g2[par, r] = jnp.sum(g1[par], axis=0)
        send_all(gram_2, par, far_col, r)
        sent_all(gram_1, par, far_row, c)

    def sum_late(par):
        recv_all(gram_2, par, far_col)
        g3[par, c] = jnp.sum(g2[par], axis=0)
        send_all(gram_3, par, far_row, c)
        sent_all(gram_2, par, far_col, r)

    def sum_end(par):
        recv_all(gram_3, par, far_row)
        sent_all(gram_3, par, far_row, c)
        return jnp.concatenate([g3[par, i] for i in range(nc)], axis=0)

    at_prev_row, at_prev_col = 0, cap
    at_last_row = 2 * cap
    at_last_col = 2 * cap + nc
    for load in load_scalars:
        load.wait()
    live = counts[0, 0]

    def latest(keys, want, below):
        found = jnp.int32(cap)
        for k in range(cap):
            hit = (keys[0, 0, k] == want) & (k < below)
            found = jnp.where(hit, k, found)
        return found

    @pl.loop(0, cap)
    def _(k):
        tab[at_prev_row + k] = latest(rows, rows[0, 0, k], k)
        tab[at_prev_col + k] = latest(cols, cols[0, 0, k], k)

    @pl.loop(0, nc)
    def _(i):
        tab[at_last_row + i] = latest(rows, i, live)

    @pl.loop(0, nr)
    def _(i):
        tab[at_last_col + i] = latest(cols, i, live)

    load_start.wait()
    v_s[...] = start[...]
    q_s[...] = jnp.zeros_like(q_s)
    qs_s[...] = jnp.zeros_like(qs_s)
    gain_s[...] = jnp.zeros_like(gain_s)
    scol[cap] = jnp.zeros(scol.shape[1:], F32)
    srow[cap] = jnp.zeros(srow.shape[1:], F32)
    load_vals.wait()
    for k in range(cap):
        vals_t[k] = vals[k].T
    pl.semaphore_wait(barrier, nr + nc - 2)

    def coefficients(total, turn):
        a = total[:, :width]
        g = total[:, width:]
        upper, inverse = factor(g - mm_nt(a, a))
        row = lax.broadcasted_iota(jnp.int32, a.shape, 0)
        lane = lax.broadcasted_iota(jnp.int32, a.shape, 1)
        here = jnp.maximum(turn, 0)
        diag_o[here] = a + (row == lane).astype(F32)
        off_o[here] = upper.T
        if not eager:
            square = jnp.sum(jnp.where(row == lane, g, 0.0), axis=0, keepdims=True)
            gain = inverse * inverse * (square / width)
            gain = jnp.sum(jnp.sum(gain, axis=1, keepdims=True), axis=0, keepdims=True)
            gain_s[...] = jnp.maximum(gain_s[...], gain)
        return a, upper, inverse

    def step(turn, _):
        par = lax.rem(turn, 2)
        v = v_s[...]
        gram = mm_nt(v, jnp.concatenate([q_s[...], v], axis=0))
        if eager:
            sum_begin(par, gram)
            sum_middle(par)
            sum_late(par)
            a, upper, inverse = coefficients(sum_end(par), turn - 1)
            q = q_s[...]
            v = mm(inverse, v - mm(a, q))
            q_s[...] = v
            qp_s[...] = mm(upper, q)
        narrow = v.astype(BF)
        xrow[par, c] = narrow
        xcol[par, r] = narrow
        if not eager:
            sum_begin(par, gram)

        for at in far_chip:
            ag_row(par, at * 2 + core, c).start()

        ag_pass(par, chip).start()

        @pl.loop(0, r)
        def _(to):
            ag_col(par, to, r).start()

        if not eager:
            sum_middle(par)

        for at in reversed(far_chip):
            ag_row(par, at * 2 + core, at * 2 + core).wait_recv()
            ag_pass(par, at).start()

        @pl.loop(0, chips)
        def _(i):
            ag_passed(par, on_chip(i)).wait_recv()

        wrow[...] = xrow[par]
        for k in range(cap):
            term = jnp.dot(
                wrow[rows[0, 0, k]], vals[k], preferred_element_type=F32
            )
            scol[k] = term + scol[tab[at_prev_col + k]]
        for i in range(nr):
            pcol[i] = scol[tab[at_last_col + i]].astype(BF)
        rcol[par, r] = pcol[r]

        @pl.loop(0, nr - 1 - r)
        def _(i):
            rs_col(par, nr - 1 - i, r).start()

        @pl.loop(r + 1, nr)
        def _(i):
            ag_col(par, i, i).wait_recv()

        wcol[...] = xcol[par]
        for k in range(cap):
            term = jnp.dot(
                wcol[cols[0, 0, k]], vals_t[k], preferred_element_type=F32
            )
            srow[k] = term + srow[tab[at_prev_row + k]]
        for i in range(chips):
            at = at_last_row + on_chip(i + 1) * 2
            psib[i] = srow[tab[at + 1 - core]].astype(BF)
            pown[i] = srow[tab[at + core]]
            rs_sib(par, i).start()

        if not eager:
            sum_late(par)

        for i in range(chips):
            rs_sib(par, i).wait_recv()
            both = pown[i] + rsib[par, i].astype(F32)
            if i < chips - 1:
                pfin[i] = both.astype(BF)
                rs_row(par, i, on_chip(i + 1), chip).start()
            else:
                rrow[par, chip] = both.astype(BF)

        if not eager:
            a, upper, inverse = coefficients(sum_end(par), turn - 1)
            q = q_s[...]
            q_s[...] = v_s[...] - mm(a, q)
            qs_s[...] = mm(a, qs_s[...])
            qp_s[...] = mm(upper, q)
            e_s[...] = inverse

        @pl.loop(0, chips - 1)
        def _(i):
            rs_row(par, i, on_chip(i + 1), on_chip(i + 1)).wait_recv()

        @pl.loop(0, r)
        def _(i):
            rs_col(par, i, i).wait_recv()

        share = jnp.sum(rrow[par].astype(F32), axis=0) + jnp.sum(
            rcol[par].astype(F32), axis=0
        )

        if eager:
            v_s[...] = -share - qp_s[...]
        else:
            both = jnp.concatenate([share - qs_s[...], q_s[...]], axis=1)
            both = mm(e_s[...], both)
            image = both[:, :edge]
            qs_s[...] = image
            v_s[...] = -image - qp_s[...]
            q_s[...] = both[:, edge:]

        @pl.loop(1, chips)
        def _(i):
            ag_row(par, on_chip(i) * 2 + core, c).wait_send()

        @pl.loop(0, chips)
        def _(i):
            ag_pass(par, i).wait_send()
            rs_sib(par, i).wait_send()

        @pl.loop(0, chips - 1)
        def _(i):
            rs_row(par, i, on_chip(i + 1), chip).wait_send()

        @pl.loop(0, r)
        def _(to):
            ag_col(par, to, r).wait_send()

        @pl.loop(0, nr - 1 - r)
        def _(i):
            rs_col(par, nr - 1 - i, r).wait_send()

        return 0

    lax.fori_loop(0, STEPS, step, 0)

    v = v_s[...]
    q = q_s[...]
    sum_begin(0, mm_nt(v, jnp.concatenate([q, v], axis=0)))
    sum_middle(0)
    sum_late(0)
    a, _, inverse = coefficients(sum_end(0), STEPS - 1)
    basis_o[...] = mm(inverse, v - mm(a, q))
    gain_o[0] = jnp.max(gain_s[...])


def lanczos(eager, counts, block_rows, block_cols, values, start_block):
    nr = lax.axis_size("row")
    nc = lax.axis_size("col")
    cap, edge, _ = values.shape[2:]
    width = start_block.shape[0]
    part = width // nc
    chips = nc // 2
    vmem = pl.BlockSpec(memory_space=pltpu.VMEM)
    hbm = pl.BlockSpec(memory_space=pltpu.HBM)
    dma = pltpu.SemaphoreType.DMA

    def block(*lead, dtype=BF):
        return pltpu.VMEM((*lead, width, edge), dtype)

    def piece(*lead):
        return pltpu.VMEM((*lead, part, 2 * width), F32)

    return pl.pallas_call(
        functools.partial(kernel, eager, nr, nc),
        out_shape=(
            jax.ShapeDtypeStruct((STEPS, width, width), F32),
            jax.ShapeDtypeStruct((STEPS, width, width), F32),
            jax.ShapeDtypeStruct((width, edge), F32),
            jax.ShapeDtypeStruct((1,), F32),
        ),
        in_specs=[hbm] * 5,
        out_specs=(vmem, vmem, vmem, pl.BlockSpec(memory_space=pltpu.SMEM)),
        scratch_shapes=[
            pltpu.SMEM(counts.shape, jnp.int32),
            pltpu.SMEM(block_rows.shape, jnp.int32),
            pltpu.SMEM(block_cols.shape, jnp.int32),
            pltpu.SMEM((2 * cap + nc + nr,), jnp.int32),
            pltpu.VMEM((cap, edge, edge), BF),
            block(dtype=F32),
            pltpu.VMEM((cap, edge, edge), BF),
            block(2, nr),
            block(2, nc),
            block(nr),
            block(nc),
            block(cap + 1, dtype=F32),
            block(cap + 1, dtype=F32),
            block(nr),
            block(chips),
            block(chips, dtype=F32),
            block(chips),
            block(2, nr),
            block(2, chips),
            block(2, chips),
            piece(nc),
            piece(2, nc),
            piece(2, nr),
            piece(2, nc),
            block(dtype=F32),
            block(dtype=F32),
            block(dtype=F32),
            block(dtype=F32),
            pltpu.VMEM((width, width), F32),
            pltpu.VMEM((8, 128), F32),
            dma((5,)),
            dma((nr,)),
            dma((2, nr)),
            dma((nc + chips,)),
            dma((2, nc)),
            dma((nr,)),
            dma((2, nr)),
            dma((chips,)),
            dma((2, chips)),
            dma((chips,)),
            dma((2, chips)),
            dma((nc,)),
            dma((2, nc)),
            dma((nr,)),
            dma((2, nr)),
            dma((nc,)),
            dma((2, nc)),
        ],
        compiler_params=pltpu.CompilerParams(
            collective_id=int(eager), has_side_effects=True, vmem_limit_bytes=60 << 20
        ),
        name="eager" if eager else "lanczos",
    )(counts, block_rows, block_cols, values, start_block)


GAIN = 2.0


def per_device(*args):
    *outs, gain = lanczos(False, *args)
    return lax.cond(
        gain[0] <= GAIN, lambda: tuple(outs), lambda: tuple(lanczos(True, *args)[:3])
    )


def solution(mesh):
    in_specs = (
        P("row", "col"),
        P("row", "col", None),
        P("row", "col", None),
        P("row", "col", None, None, None),
        P(None, ("row", "col")),
    )
    out_specs = (P(), P(), P(None, ("row", "col")))
    return jax.shard_map(
        per_device, mesh=mesh, in_specs=in_specs, out_specs=out_specs, check_vma=False
    )
```

```python
import functools

import jax
import jax.numpy as jnp
from jax import lax
from jax.experimental import pallas as pl
from jax.experimental.pallas import tpu as pltpu
from jax.sharding import PartitionSpec as P

STEPS = 4
HI = lax.Precision.HIGHEST
F32 = jnp.float32
BF = jnp.bfloat16
MESH = pl.DeviceIdType.MESH


def mm(a, b):
    return lax.dot_general(
        a, b, (((1,), (0,)), ((), ())), precision=HI, preferred_element_type=F32
    )


def mm_nt(a, b):
    return lax.dot_general(
        a, b, (((1,), (1,)), ((), ())), precision=HI, preferred_element_type=F32
    )


GROUP = 8


def factor(gram):
    n = gram.shape[0]
    row = lax.broadcasted_iota(jnp.int32, (n, 2 * n), 0)
    lane = lax.broadcasted_iota(jnp.int32, (n, 2 * n), 1)
    eye = (row[:, :n] == lane[:, :n]).astype(F32)
    m = jnp.concatenate([gram, eye], axis=1)
    above = lax.broadcasted_iota(jnp.int32, (GROUP, 2 * n), 0)
    done = []
    for first in range(0, n, GROUP):
        cols = [
            jnp.broadcast_to(m[:, first + j : first + j + 1], m.shape)
            for j in range(GROUP)
        ]
        for j in range(GROUP):
            inverse = 1.0 / cols[j][j : j + 1]
            head = jnp.where(above > j, cols[j][:GROUP], 0.0)
            mult = head if m.shape[0] == GROUP else jnp.concatenate(
                [head, cols[j][GROUP:]], axis=0
            )
            mult = mult * inverse
            for i in range(j + 1, GROUP):
                cols[i] = cols[i] - mult * cols[i][j : j + 1]
            m = m - mult * m[j : j + 1]
        done.append(m[:GROUP])
        m = m[GROUP:]
    m = jnp.concatenate(done, axis=0)
    diag = jnp.sum(jnp.where(row == lane, m, 0.0), axis=1, keepdims=True)
    m = m / jnp.sqrt(diag)
    upper = jnp.where(lane[:, :n] >= row[:, :n], m[:, :n], 0.0)
    return upper, m[:, n:]


def kernel(
    eager,
    nr,
    nc,
    counts_hbm,
    rows_hbm,
    cols_hbm,
    vals_hbm,
    start_hbm,
    diag_o,
    off_o,
    basis_o,
    gain_o,
    counts,
    rows,
    cols,
    tab,
    vals,
    start,
    vals_t,
    xcol,
    xrow,
    wcol,
    wrow,
    scol,
    srow,
    pcol,
    psib,
    pown,
    pfin,
    rcol,
    rsib,
    rrow,
    ga,
    g1,
    g2,
    g3,
    q_s,
    qs_s,
    qp_s,
    v_s,
    e_s,
    gain_s,
    load_sem,
    ax_send,
    ax_recv,
    ay_send,
    ay_recv,
    bx_send,
    bx_recv,
    bs_send,
    bs_recv,
    by_send,
    by_recv,
    g1_send,
    g1_recv,
    g2_send,
    g2_recv,
    g3_send,
    g3_recv,
):
    cap = vals.shape[0]
    width, edge = start.shape
    part = width // nc
    chips = nc // 2
    r = lax.axis_index("row")
    c = lax.axis_index("col")
    core = lax.rem(c, 2)
    chip = c // 2
    other = chip * 2 + 1 - core

    load_start = pltpu.make_async_copy(start_hbm, start, load_sem.at[0])
    load_vals = pltpu.make_async_copy(vals_hbm.at[0, 0], vals, load_sem.at[1])
    load_scalars = [
        pltpu.make_async_copy(src, dst, load_sem.at[2 + i])
        for i, (src, dst) in enumerate(
            ((counts_hbm, counts), (rows_hbm, rows), (cols_hbm, cols))
        )
    ]
    load_start.start()
    for load in load_scalars:
        load.start()
    load_vals.start()

    def on_col(i):
        return lax.rem(r + i, nr)

    def on_row(i):
        return lax.rem(c + i, nc)

    def on_chip(i):
        return lax.rem(chip + i, chips)

    xcol[...] = jnp.zeros_like(xcol)
    rcol[...] = jnp.zeros_like(rcol)

    barrier = pltpu.get_barrier_semaphore()

    @pl.loop(1, nr)
    def _(i):
        pl.semaphore_signal(
            barrier, inc=1, device_id=(on_col(i), c), device_id_type=MESH
        )

    @pl.loop(1, nc)
    def _(i):
        pl.semaphore_signal(
            barrier, inc=1, device_id=(r, on_row(i)), device_id_type=MESH
        )

    def remote(src, dst, send, recv, device):
        return pltpu.make_async_remote_copy(
            src_ref=src,
            dst_ref=dst,
            send_sem=send,
            recv_sem=recv,
            device_id=device,
            device_id_type=MESH,
        )

    def ag_col(par, to, slot):
        return remote(
            xcol.at[par, r],
            xcol.at[par, slot],
            ax_send.at[to],
            ax_recv.at[par, slot],
            (to, c),
        )

    def ag_row(par, to, slot):
        return remote(
            xrow.at[par, slot],
            xrow.at[par, slot],
            ay_send.at[to],
            ay_recv.at[par, slot],
            (r, to),
        )

    def ag_pass(par, at):
        return remote(
            xrow.at[par, at * 2 + core],
            xrow.at[par, at * 2 + core],
            ay_send.at[nc + at],
            ay_recv.at[par, at * 2 + core],
            (r, other),
        )

    def ag_passed(par, at):
        return remote(
            xrow.at[par, at * 2 + 1 - core],
            xrow.at[par, at * 2 + 1 - core],
            ay_send.at[nc + at],
            ay_recv.at[par, at * 2 + 1 - core],
            (r, other),
        )

    def rs_col(par, to, slot):
        return remote(
            pcol.at[to],
            rcol.at[par, slot],
            bx_send.at[to],
            bx_recv.at[par, slot],
            (to, c),
        )

    def rs_sib(par, i):
        return remote(
            psib.at[i],
            rsib.at[par, i],
            bs_send.at[i],
            bs_recv.at[par, i],
            (r, other),
        )

    def rs_row(par, i, to, slot):
        return remote(
            pfin.at[i],
            rrow.at[par, slot],
            by_send.at[i],
            by_recv.at[par, slot],
            (r, to * 2 + core),
        )

    def gram_1(par, to, slot):
        return remote(
            ga.at[to],
            g1.at[par, slot],
            g1_send.at[to],
            g1_recv.at[par, slot],
            (r, to),
        )

    def gram_2(par, to, slot):
        return remote(
            g2.at[par, r],
            g2.at[par, slot],
            g2_send.at[to],
            g2_recv.at[par, slot],
            (to, c),
        )

    def gram_3(par, to, slot):
        return remote(
            g3.at[par, c],
            g3.at[par, slot],
            g3_send.at[to],
            g3_recv.at[par, slot],
            (r, to),
        )

    nx = min(4, chips)
    ny = chips // nx
    y, x = chip // nx, lax.rem(chip, nx)

    def ring(d, n):
        return min(d, n - d)

    plane = sorted(
        (
            (dy, dx, dc)
            for dy in range(ny)
            for dx in range(nx)
            for dc in range(2)
            if (dy, dx, dc) != (0, 0, 0)
        ),
        key=lambda o: -(10 * (ring(o[0], ny) + ring(o[1], nx)) + o[2]),
    )
    far_row = []
    for dy, dx, dc in plane:
        at = lax.rem(y + dy, ny) * nx + lax.rem(x + dx, nx)
        far_row.append(at * 2 + (core if dc == 0 else 1 - core))
    far_chip = [at for dy, dx, dc in plane if dc == 0 for at in (
        lax.rem(y + dy, ny) * nx + lax.rem(x + dx, nx),)]
    far = sorted(range(1, nr), key=lambda d: -ring(d, nr))
    far_col = [on_col(d) for d in far]

    def send_all(copy, par, peers, me):
        for to in peers:
            copy(par, to, me).start()

    def recv_all(copy, par, peers):
        for to in reversed(peers):
            copy(par, to, to).wait_recv()

    def sent_all(copy, par, peers, me):
        for to in peers:
            copy(par, to, me).wait_send()

    def sum_begin(par, whole):
        for i in range(nc):
            ga[i] = whole[i * part : (i + 1) * part]
        g1[par, c] = ga[c]
        send_all(gram_1, par, far_row, c)

    def sum_middle(par):
        recv_all(gram_1, par, far_row)
        g2[par, r] = jnp.sum(g1[par], axis=0)
        send_all(gram_2, par, far_col, r)

    def sum_late(par):
        recv_all(gram_2, par, far_col)
        g3[par, c] = jnp.sum(g2[par], axis=0)
        send_all(gram_3, par, far_row, c)

    def sum_end(par):
        recv_all(gram_3, par, far_row)
        return jnp.concatenate([g3[par, i] for i in range(nc)], axis=0)

    at_prev_row, at_prev_col = 0, cap
    at_last_row = 2 * cap
    at_last_col = 2 * cap + nc
    for load in load_scalars:
        load.wait()
    live = counts[0, 0]

    def latest(keys, want, below):
        found = jnp.int32(cap)
        for k in range(cap):
            hit = (keys[0, 0, k] == want) & (k < below)
            found = jnp.where(hit, k, found)
        return found

    @pl.loop(0, cap)
    def _(k):
        tab[at_prev_row + k] = latest(rows, rows[0, 0, k], k)
        tab[at_prev_col + k] = latest(cols, cols[0, 0, k], k)

    @pl.loop(0, nc)
    def _(i):
        tab[at_last_row + i] = latest(rows, i, live)

    @pl.loop(0, nr)
    def _(i):
        tab[at_last_col + i] = latest(cols, i, live)

    load_start.wait()
    v_s[...] = start[...]
    q_s[...] = jnp.zeros_like(q_s)
    qs_s[...] = jnp.zeros_like(qs_s)
    gain_s[...] = jnp.zeros_like(gain_s)
    scol[cap] = jnp.zeros(scol.shape[1:], F32)
    srow[cap] = jnp.zeros(srow.shape[1:], F32)
    load_vals.wait()
    for k in range(cap):
        vals_t[k] = vals[k].T
    pl.semaphore_wait(barrier, nr + nc - 2)

    def coefficients(total, turn):
        a = total[:, :width]
        g = total[:, width:]
        upper, inverse = factor(g - mm_nt(a, a))
        row = lax.broadcasted_iota(jnp.int32, a.shape, 0)
        lane = lax.broadcasted_iota(jnp.int32, a.shape, 1)
        here = jnp.maximum(turn, 0)
        diag_o[here] = a + (row == lane).astype(F32)
        off_o[here] = upper.T
        if not eager:
            square = jnp.sum(jnp.where(row == lane, g, 0.0), axis=0, keepdims=True)
            gain = inverse * inverse * (square / width)
            gain = jnp.sum(jnp.sum(gain, axis=1, keepdims=True), axis=0, keepdims=True)
            gain_s[...] = jnp.maximum(gain_s[...], gain)
        return a, upper, inverse

    def sent_last(par):
        if not eager:
            sent_all(gram_3, par, far_row, c)

        @pl.loop(0, chips)
        def _(i):
            rs_sib(par, i).wait_send()

        for i in range(chips - 1):
            rs_row(par, i, far_chip[i], chip).wait_send()

        @pl.loop(0, nr - 1 - r)
        def _(i):
            rs_col(par, nr - 1 - i, r).wait_send()

    def step(turn, _):
        par = lax.rem(turn, 2)
        v = v_s[...]
        if eager:
            gram = mm_nt(v, jnp.concatenate([q_s[...], v], axis=0))
            sum_begin(par, gram)
            sum_middle(par)
            sum_late(par)
            a, upper, inverse = coefficients(sum_end(par), turn - 1)
            q = q_s[...]
            v = mm(inverse, v - mm(a, q))
            q_s[...] = v
            qp_s[...] = mm(upper, q)
            sent_all(gram_1, par, far_row, c)
            sent_all(gram_2, par, far_col, r)
            sent_all(gram_3, par, far_row, c)
        narrow = v.astype(BF)
        xrow[par, c] = narrow
        xcol[par, r] = narrow
        for d in far:

            @pl.when(r >= d)
            def _():
                ag_col(par, r - d, r).start()

        if not eager:
            sum_begin(par, mm_nt(v, jnp.concatenate([q_s[...], v], axis=0)))

        for at in far_chip:
            ag_row(par, at * 2 + core, c).start()

        ag_pass(par, chip).start()

        if not eager:
            sum_middle(par)

        for at in reversed(far_chip):
            ag_row(par, at * 2 + core, at * 2 + core).wait_recv()
            ag_pass(par, at).start()

        @pl.when(turn > 0)
        def _():
            sent_last(1 - par)

        @pl.loop(0, chips)
        def _(i):
            ag_passed(par, on_chip(i)).wait_recv()

        wrow[...] = xrow[par]
        for k in range(cap):
            term = jnp.dot(
                wrow[rows[0, 0, k]], vals[k], preferred_element_type=F32
            )
            scol[k] = term + scol[tab[at_prev_col + k]]
        for i in range(nr):
            pcol[i] = scol[tab[at_last_col + i]].astype(BF)
        rcol[par, r] = pcol[r]

        for d in far:

            @pl.when(r + d < nr)
            def _():
                rs_col(par, r + d, r).start()

        for at in far_chip:
            ag_row(par, at * 2 + core, c).wait_send()

        @pl.loop(0, chips)
        def _(i):
            ag_pass(par, i).wait_send()

        if not eager:
            sent_all(gram_1, par, far_row, c)

        @pl.loop(r + 1, nr)
        def _(i):
            ag_col(par, i, i).wait_recv()

        wcol[...] = xcol[par]
        for k in range(cap):
            term = jnp.dot(
                wcol[cols[0, 0, k]], vals_t[k], preferred_element_type=F32
            )
            srow[k] = term + srow[tab[at_prev_row + k]]
        for i in range(chips):
            at = at_last_row + ([*far_chip, chip])[i] * 2
            psib[i] = srow[tab[at + 1 - core]].astype(BF)
            pown[i] = srow[tab[at + core]]
            rs_sib(par, i).start()

        if not eager:
            sum_late(par)

        for i in range(chips):
            rs_sib(par, i).wait_recv()
            both = pown[i] + rsib[par, i].astype(F32)
            if i < chips - 1:
                pfin[i] = both.astype(BF)
                rs_row(par, i, far_chip[i], chip).start()
            else:
                rrow[par, chip] = both.astype(BF)

        @pl.loop(0, r)
        def _(to):
            ag_col(par, to, r).wait_send()

        if not eager:
            sent_all(gram_2, par, far_col, r)
            a, upper, inverse = coefficients(sum_end(par), turn - 1)
            q = q_s[...]
            q_s[...] = v_s[...] - mm(a, q)
            qs_s[...] = mm(a, qs_s[...])
            qp_s[...] = mm(upper, q)
            e_s[...] = inverse

        for i in reversed(range(chips - 1)):
            rs_row(par, i, far_chip[i], far_chip[i]).wait_recv()

        @pl.loop(0, r)
        def _(i):
            rs_col(par, i, i).wait_recv()

        share = jnp.sum(rrow[par].astype(F32), axis=0) + jnp.sum(
            rcol[par].astype(F32), axis=0
        )

        if eager:
            v_s[...] = -share - qp_s[...]
        else:
            both = jnp.concatenate([share - qs_s[...], q_s[...]], axis=1)
            both = mm(e_s[...], both)
            image = both[:, :edge]
            qs_s[...] = image
            v_s[...] = -image - qp_s[...]
            q_s[...] = both[:, edge:]

        return 0

    lax.fori_loop(0, STEPS, step, 0)

    v = v_s[...]
    q = q_s[...]
    sum_begin(0, mm_nt(v, jnp.concatenate([q, v], axis=0)))
    sent_last((STEPS - 1) % 2)
    sum_middle(0)
    sum_late(0)
    a, _, inverse = coefficients(sum_end(0), STEPS - 1)
    basis_o[...] = mm(inverse, v - mm(a, q))
    gain_o[0] = jnp.max(gain_s[...])
    sent_all(gram_1, 0, far_row, c)
    sent_all(gram_2, 0, far_col, r)
    sent_all(gram_3, 0, far_row, c)


def lanczos(eager, counts, block_rows, block_cols, values, start_block):
    nr = lax.axis_size("row")
    nc = lax.axis_size("col")
    cap, edge, _ = values.shape[2:]
    width = start_block.shape[0]
    part = width // nc
    chips = nc // 2
    vmem = pl.BlockSpec(memory_space=pltpu.VMEM)
    hbm = pl.BlockSpec(memory_space=pltpu.HBM)
    dma = pltpu.SemaphoreType.DMA

    def block(*lead, dtype=BF):
        return pltpu.VMEM((*lead, width, edge), dtype)

    def piece(*lead):
        return pltpu.VMEM((*lead, part, 2 * width), F32)

    return pl.pallas_call(
        functools.partial(kernel, eager, nr, nc),
        out_shape=(
            jax.ShapeDtypeStruct((STEPS, width, width), F32),
            jax.ShapeDtypeStruct((STEPS, width, width), F32),
            jax.ShapeDtypeStruct((width, edge), F32),
            jax.ShapeDtypeStruct((1,), F32),
        ),
        in_specs=[hbm] * 5,
        out_specs=(vmem, vmem, vmem, pl.BlockSpec(memory_space=pltpu.SMEM)),
        scratch_shapes=[
            pltpu.SMEM(counts.shape, jnp.int32),
            pltpu.SMEM(block_rows.shape, jnp.int32),
            pltpu.SMEM(block_cols.shape, jnp.int32),
            pltpu.SMEM((2 * cap + nc + nr,), jnp.int32),
            pltpu.VMEM((cap, edge, edge), BF),
            block(dtype=F32),
            pltpu.VMEM((cap, edge, edge), BF),
            block(2, nr),
            block(2, nc),
            block(nr),
            block(nc),
            block(cap + 1, dtype=F32),
            block(cap + 1, dtype=F32),
            block(nr),
            block(chips),
            block(chips, dtype=F32),
            block(chips),
            block(2, nr),
            block(2, chips),
            block(2, chips),
            piece(nc),
            piece(2, nc),
            piece(2, nr),
            piece(2, nc),
            block(dtype=F32),
            block(dtype=F32),
            block(dtype=F32),
            block(dtype=F32),
            pltpu.VMEM((width, width), F32),
            pltpu.VMEM((8, 128), F32),
            dma((5,)),
            dma((nr,)),
            dma((2, nr)),
            dma((nc + chips,)),
            dma((2, nc)),
            dma((nr,)),
            dma((2, nr)),
            dma((chips,)),
            dma((2, chips)),
            dma((chips,)),
            dma((2, chips)),
            dma((nc,)),
            dma((2, nc)),
            dma((nr,)),
            dma((2, nr)),
            dma((nc,)),
            dma((2, nc)),
        ],
        compiler_params=pltpu.CompilerParams(
            collective_id=int(eager), has_side_effects=True, vmem_limit_bytes=60 << 20
        ),
        name="eager" if eager else "lanczos",
    )(counts, block_rows, block_cols, values, start_block)


GAIN = 2.0


def per_device(*args):
    *outs, gain = lanczos(False, *args)
    return lax.cond(
        gain[0] <= GAIN, lambda: tuple(outs), lambda: tuple(lanczos(True, *args)[:3])
    )


def solution(mesh):
    in_specs = (
        P("row", "col"),
        P("row", "col", None),
        P("row", "col", None),
        P("row", "col", None, None, None),
        P(None, ("row", "col")),
    )
    out_specs = (P(), P(), P(None, ("row", "col")))
    return jax.shard_map(
        per_device, mesh=mesh, in_specs=in_specs, out_specs=out_specs, check_vma=False
    )
```
